512 devices in a mesh: section: 16 (over y, x), expert: 32 (over z, core).
Axes of the slice: x: 4, y: 4, z: 16, core: 2. Of those that a mesh axis runs over, the one named last changes fastest.
Arguments:
- activations: bfloat16 [16, 4096, 2048], P('section', 'expert'), may hold values from -6 to 6
- norm_gain: float32 [16, 2048], P('section'), may hold values from 0.1 to 1.9
- router: bfloat16 [16, 2048, 8], P('section'), may hold values from -0.125 to 0.125
- expert_in: bfloat16 [16, 32, 2048, 512], P('section', 'expert'), may hold values from -0.125 to 0.125
- expert_down: bfloat16 [16, 32, 256, 2048], P('section', 'expert'), may hold values from -0.1875 to 0.1875
- expert_ids: int32 [2, 16, 4096], P(None, 'section', 'expert'), may hold values from 0 to 7, as said below
- slot_ids: int32 [2, 16, 4096], P(None, 'section', 'expert'), may hold values from 0 to 23, as said below
Outputs:
- carried: bfloat16 [16, 4096, 2048], P('section', 'expert')
The draws below stay inside these ranges and needn't reach their ends.
Inputs may be any that keep to these rules, and one draw needn't show every extreme that they name: `expert_ids`: in each aligned block of 128 tokens at one stop and section, no two tokens share both expert and slot, and some expert has all 24 of its slots taken. `slot_ids`: slot of the token within the tile of its block and expert.
All inputs are finite; a program needn't handle non-finite values.
Results may differ from the reference program's by a relative error of at most 0.006.
Values may be sent and summed in bfloat16 or wider, within the bound.
A program may use at most 64 MiB of HBM per device.

```python
import jax
import jax.numpy as jnp
from jax import lax

D = 2048
FF = 1024
SPLIT = 4
STEPS = 2
TOK_DEV = 128
FF_DEV = 256
EXPERTS = 8
CAP = 24
TOKENS = 4096
N_SECTION = 16
N_EXPERT = 32


def route_cells(key):
    block_count = STEPS * N_SECTION * N_EXPERT
    cell_count = EXPERTS * CAP
    key_hot, key_level, key_noise, key_order = jax.random.split(key, 4)
    hot_expert = jax.random.randint(key_hot, (block_count, 1), 0, EXPERTS)
    level = jax.random.randint(key_level, (STEPS * N_SECTION, EXPERTS), 0, 4)
    level = jnp.repeat(level, N_EXPERT, axis=0)
    owner = jnp.arange(cell_count, dtype=jnp.int32) // CAP
    level_cells = level[:, owner]
    noise = jax.random.randint(key_noise, (block_count, cell_count), 0, 16384)
    score = noise + level_cells * 4096 + jnp.where(owner[None, :] == hot_expert, 65536, 0)
    distinct = score * cell_count + jnp.arange(cell_count, dtype=jnp.int32)[None, :]
    unused, chosen = lax.top_k(distinct, TOK_DEV)
    shuffle = jax.random.randint(key_order, (block_count, TOK_DEV), 0, 65536) * TOK_DEV + jnp.arange(TOK_DEV, dtype=jnp.int32)[None, :]
    order = jnp.argsort(shuffle, axis=1, stable=True)
    chosen = jnp.take_along_axis(chosen, order, axis=1)
    return chosen.reshape(STEPS, N_SECTION, N_EXPERT * TOK_DEV).astype(jnp.int32)


def draw_expert_ids(key, part):
    return (route_cells(key) // CAP).astype(jnp.int32)


def draw_slot_ids(key, part):
    return (route_cells(key) % CAP).astype(jnp.int32)


def steps_of(key, shape, cuts, smallest, largest):
    gain = 1.0
    for dim, parts in cuts:
        draws = jax.random.uniform(jax.random.fold_in(jax.random.fold_in(key, 6), dim), (parts,), jnp.float32, smallest / len(cuts), largest / len(cuts))
        gain = gain * jnp.repeat(jnp.exp(draws), shape[dim] // parts).reshape((-1,) + (1,) * (len(shape) - 1 - dim))
    return gain


def normal_values(rng, extent, scale, reach, cuts=(), kind=jnp.bfloat16):
    gain = steps_of(rng, extent, cuts, -0.22, 0.18) if cuts else 1.0
    array = jax.random.normal(rng, extent, jnp.float32) * scale * gain
    return jnp.minimum(jnp.maximum(array, -reach), reach).astype(kind)


def setup_inputs(seed: int = 0) -> dict:
    seeds = jax.random.split(jax.random.key(seed), 8)
    activations = normal_values(seeds[0], (N_SECTION, TOKENS, D), 1.0, 6.0, ((0, 16), (1, 32)))
    norm_gain = jnp.clip(1.0 + 0.18 * jax.random.normal(seeds[1], (N_SECTION, D), jnp.float32), 0.1, 1.9)
    router = normal_values(seeds[2], (N_SECTION, D, EXPERTS), D ** -0.5, 0.125, ((0, 16),))
    expert_in = normal_values(seeds[3], (N_SECTION, N_EXPERT, D, 2 * FF_DEV), D ** -0.5, 0.125, ((0, 16), (1, 32)))
    expert_down = normal_values(seeds[4], (N_SECTION, N_EXPERT, FF_DEV, D), FF ** -0.5, 0.1875, ((0, 16), (1, 32)))
    expert_ids = draw_expert_ids(jax.random.fold_in(seeds[7], 71), 0)
    slot_ids = draw_slot_ids(jax.random.fold_in(seeds[7], 71), 0)
    return {"activations": activations, "norm_gain": norm_gain, "router": router, "expert_in": expert_in, "expert_down": expert_down, "expert_ids": expert_ids, "slot_ids": slot_ids}


def through_expert(packed):
    row_block, in_weights, down_weights = packed
    hidden_width = down_weights.shape[1]
    running = jnp.zeros((row_block.shape[0], row_block.shape[1]), jnp.float32)
    for member in range(in_weights.shape[0]):
        projected = jnp.dot(row_block, in_weights[member], preferred_element_type=jnp.float32)
        hidden = (jax.nn.silu(projected[:, :hidden_width]) * projected[:, hidden_width:]).astype(jnp.bfloat16)
        partial_value = jnp.dot(hidden, down_weights[member], preferred_element_type=jnp.float32).astype(jnp.bfloat16)
        running = running + lax.optimization_barrier(partial_value).astype(jnp.float32)
    return running.astype(jnp.bfloat16)

def section_layer(packed):
    current, gain_row, router_matrix, in_weights, down_weights, chosen, slot_row = packed
    wide_rows = current.astype(jnp.float32)
    inverse_rms = lax.rsqrt(lax.optimization_barrier(jnp.mean(wide_rows * wide_rows, axis=-1, keepdims=True)) + 1e-06)
    normed = (wide_rows * inverse_rms * gain_row[None, :]).astype(jnp.bfloat16)
    logits = jnp.dot(normed, router_matrix, preferred_element_type=jnp.float32)
    picked = jnp.take_along_axis(logits, chosen[:, None].astype(jnp.int32), axis=1)
    weight = jax.nn.sigmoid(picked)
    block_index = jnp.arange(TOKENS, dtype=jnp.int32) // TOK_DEV
    target_row = ((block_index * EXPERTS + chosen) * CAP + slot_row).astype(jnp.int32)
    expert_tiles = jnp.zeros((N_EXPERT * EXPERTS * CAP, D), jnp.bfloat16).at[target_row].set(normed)
    grouped = expert_tiles.reshape(N_EXPERT, EXPERTS, CAP, D).transpose(1, 0, 2, 3).reshape(EXPERTS, N_EXPERT * CAP, D)
    in_grouped = in_weights.reshape(EXPERTS, SPLIT, D, 2 * FF_DEV)
    down_grouped = down_weights.reshape(EXPERTS, SPLIT, FF_DEV, D)
    results = lax.map(through_expert, (grouped, in_grouped, down_grouped))
    returned = results.reshape(EXPERTS, N_EXPERT, CAP, D).transpose(1, 0, 2, 3).reshape(N_EXPERT * EXPERTS * CAP, D)
    gathered = returned[target_row].astype(jnp.float32)
    return (wide_rows + weight * gathered).astype(jnp.bfloat16)

def reference(activations, norm_gain, router, expert_in, expert_down, expert_ids, slot_ids):
    carried = activations
    for stop_index in range(STEPS):
        carried = lax.map(section_layer, (carried, norm_gain, router, expert_in, expert_down, expert_ids[stop_index], slot_ids[stop_index]))
        carried = jnp.roll(carried, 1, axis=0)
    return carried
```

```python
import functools

import jax
import jax.numpy as jnp
from jax import lax
from jax.experimental import pallas as pl
from jax.experimental.pallas import tpu as pltpu
from jax.sharding import PartitionSpec as P

STEPS = 2
CAP = 24
TOK = 128
SPLIT = 4
MESH = pl.DeviceIdType.MESH
LAND, TO_SIBLING, TO_PARTNER, TO_BOTH, PART_SIBLING, PART_FAR, PART_PARTNER, RESULT, META = range(9)


def kernel(
    n_section, n_expert,
    x_ref, gain_ref, router_ref, w_in_ref, w_down_ref, ids_ref, slots_ref,
    out_ref,
    x_buf, gain, router, w_in, w_down, ids, slots,
    normed, onehot, weight, onehot_in, weight_in, x_in,
    tiles, rows, part, far_in, sib_in, pair_in, pair_out, final, result,
    gathered, local_sem, send_sem, recv_sem,
):
    f32, bf16 = jnp.float32, jnp.bfloat16
    chips = n_expert // 2
    n_tiles = n_expert // SPLIT
    width = x_buf.shape[2]
    hidden_width = w_down.shape[0]
    s = lax.axis_index("section")
    e = lax.axis_index("expert")
    z, c = e // 2, e % 2
    side = z % 2
    s_next = (s + 1) % n_section
    s_prev = (s + n_section - 1) % n_section

    def source(k):
        return (z + (2 * side - 1) * k + chips) % chips

    def target(k):
        return (z + (1 - 2 * ((z + k) % 2)) * k + chips) % chips

    sibling = (s, e + 1 - 2 * c)
    partner = (s, (z + 1 - 2 * side) * 2 + c)

    loads = [
        pltpu.make_async_copy(x_ref.at[0], x_buf.at[0], local_sem.at[0]),
        pltpu.make_async_copy(gain_ref, gain, local_sem.at[1]),
        pltpu.make_async_copy(router_ref.at[0], router, local_sem.at[2]),
        pltpu.make_async_copy(ids_ref, ids, local_sem.at[3]),
        pltpu.make_async_copy(slots_ref, slots, local_sem.at[4]),
        pltpu.make_async_copy(w_in_ref.at[0, 0], w_in, local_sem.at[5]),
        pltpu.make_async_copy(w_down_ref.at[0, 0], w_down, local_sem.at[6]),
    ]
    for load in loads:
        load.start()

    barrier = pltpu.get_barrier_semaphore()

    def greet(device):
        pl.semaphore_signal(barrier, inc=1, device_id=device, device_id_type=MESH)

    greet(sibling)
    greet(partner)

    @pl.loop(0, n_tiles)
    def _(k):
        greet((s_next, source(k) * 2 + c))
        greet((s_prev, target(k) * 2 + c))

    @pl.loop(1, n_tiles)
    def _(k):
        greet((s, source(k) * 2 + c))
        greet((s, target(k) * 2 + c))

    for load in loads[:5]:
        load.wait()

    def remote(t, kind, k, src, dst, device):
        return pltpu.make_async_remote_copy(
            src_ref=src, dst_ref=dst, send_sem=send_sem.at[t, kind, k], recv_sem=recv_sem.at[t, kind, k],
            device_id=device, device_id_type=MESH,
        )

    def land(t, k):
        return remote(t, LAND, k, tiles.at[t, k], rows.at[t, 0, k], (s, target(k) * 2 + c))

    def to_sibling(t, k):
        return remote(t, TO_SIBLING, k, rows.at[t, 0, k], rows.at[t, 1, k], sibling)

    def to_partner(t, k):
        return remote(t, TO_PARTNER, k, rows.at[t, 0, k], rows.at[t, 2, k], partner)

    def to_both(t, k):
        return remote(t, TO_BOTH, k, rows.at[t, 2, k], rows.at[t, 3, k], sibling)

    def part_sibling(t, k):
        return remote(t, PART_SIBLING, k, part.at[t, 1, k], sib_in.at[t, k], sibling)

    def part_far(t, k):
        return remote(t, PART_FAR, k, part.at[t, 3, k], far_in.at[t, k], sibling)

    def part_partner(t, k):
        return remote(t, PART_PARTNER, k, pair_out.at[t, k], pair_in.at[t, k], partner)

    def to_home(t, k):
        return remote(t, RESULT, k, final.at[t, k], result.at[t, k], (s_next, source(k) * 2 + c))

    def metas(t):
        home = (s_next, e)
        return (
            remote(t, META, 0, x_buf.at[t], x_in.at[t], home),
            remote(t, META, 1, weight.at[t], weight_in.at[t], home),
            remote(t, META, 2, onehot.at[t], onehot_in.at[t], home),
        )

    def norm_and_route(t):
        @pl.loop(0, TOK // 16)
        def _(i):
            at = pl.ds(pl.multiple_of(i * 16, 16), 16)
            wide = x_buf[t, at, :].astype(f32)
            inverse = lax.rsqrt(jnp.mean(wide * wide, axis=-1, keepdims=True) + 1e-06)
            normed[at, :] = (wide * inverse * gain[...]).astype(bf16)

        id_row = ids[t]
        row_of = id_row * CAP + slots[t]
        for k in range(n_tiles):
            owner = target(k) // 2
            place = lax.broadcasted_iota(jnp.int32, (CAP, TOK), 0) + owner * CAP
            hot = jnp.where(place == row_of, 1.0, 0.0)
            onehot[t, k] = hot.astype(bf16)

        @pl.loop(0, n_tiles)
        def _(k):
            tile = jnp.dot(onehot[t, k], normed[...], preferred_element_type=f32).astype(bf16)

            @pl.when(k == 0)
            def _():
                rows[t, 0, 0] = tile

            @pl.when(k > 0)
            def _():
                tiles[t, k] = tile

            @pl.when((k == 0) & (t == 0))
            def _():
                pl.semaphore_wait(barrier, 4 * n_tiles)

            @pl.when(k > 0)
            def _():
                land(t, k).start()

        logits = jnp.dot(normed[...], router[...], preferred_element_type=f32)
        id_column = jnp.transpose(jnp.broadcast_to(id_row.astype(f32), (TOK, TOK)))[:, : logits.shape[1]]
        lanes = lax.broadcasted_iota(jnp.int32, logits.shape, 1)
        picked = jnp.sum(jnp.where(id_column.astype(jnp.int32) == lanes, logits, 0.0), axis=1, keepdims=True)
        weight[t] = jnp.broadcast_to(jax.nn.sigmoid(picked), (TOK, TOK))
        for copy in metas(t):
            copy.start()

    def experts(t, k):
        held = jnp.concatenate([rows[t, g, k].astype(f32) for g in range(SPLIT)], axis=0).astype(bf16)
        projected = jnp.dot(held, w_in[...], preferred_element_type=f32)
        gate, up = projected[:, :hidden_width], projected[:, hidden_width:]
        hidden = (gate * jax.nn.sigmoid(gate) * up).astype(bf16)
        value = jnp.dot(hidden, w_down[...], preferred_element_type=f32)
        for g in range(SPLIT):
            part[t, g, k] = value[g * CAP : (g + 1) * CAP].astype(bf16)

    def stop(t):
        norm_and_route(t)
        if t == 0:
            for load in loads[5:]:
                load.wait()

        @pl.loop(0, n_tiles + 4)
        def _(i):
            @pl.when(i < n_tiles)
            def _():
                @pl.when(i > 0)
                def _():
                    land(t, i).wait_recv()

                to_partner(t, i).start()
                to_sibling(t, i).start()

            @pl.when((i >= 1) & (i < n_tiles + 1))
            def _():
                k = i - 1
                to_partner(t, k).wait_recv()
                to_both(t, k).start()

            @pl.when((i >= 2) & (i < n_tiles + 2))
            def _():
                k = i - 2
                to_sibling(t, k).wait_recv()
                to_both(t, k).wait_recv()
                experts(t, k)
                part_far(t, k).start()
                part_sibling(t, k).start()

            @pl.when((i >= 3) & (i < n_tiles + 3))
            def _():
                k = i - 3
                part_far(t, k).wait_recv()
                pair_out[t, k] = (part[t, 2, k].astype(f32) + far_in[t, k].astype(f32)).astype(bf16)
                part_partner(t, k).start()

            @pl.when(i >= 4)
            def _():
                k = i - 4
                part_sibling(t, k).wait_recv()
                part_partner(t, k).wait_recv()
                total = part[t, 0, k].astype(f32) + sib_in[t, k].astype(f32) + pair_in[t, k].astype(f32)
                final[t, k] = total.astype(bf16)
                to_home(t, k).start()

        for copy in metas(t):
            copy.wait_recv()

        @pl.loop(0, n_tiles)
        def _(k):
            to_home(t, k).wait_recv()
            here = lax.dot_general(
                onehot_in[t, k], result[t, k], (((0,), (0,)), ((), ())), preferred_element_type=f32
            )

            @pl.when(k == 0)
            def _():
                gathered[...] = here

            @pl.when(k > 0)
            def _():
                gathered[...] += here

        @pl.loop(0, TOK // 16)
        def _(i):
            at = pl.ds(pl.multiple_of(i * 16, 16), 16)
            mixed = x_in[t, at, :].astype(f32) + weight_in[t, at, 0:1] * gathered[at, :]
            x_buf[t + 1, at, :] = mixed.astype(bf16)

    for t in range(STEPS):
        stop(t)
    store = pltpu.make_async_copy(x_buf.at[STEPS], out_ref.at[0], local_sem.at[0])
    store.start()
    for t in range(STEPS):
        for copy in metas(t):
            copy.wait_send()

        @pl.loop(0, n_tiles)
        def _(k):
            @pl.when(k > 0)
            def _():
                land(t, k).wait_send()

            for copy in (to_sibling, to_partner, to_both, part_sibling, part_far, part_partner, to_home):
                copy(t, k).wait_send()

    store.wait()


def local(n_section, n_expert, activations, norm_gain, router, expert_in, expert_down, expert_ids, slot_ids):
    width = activations.shape[2]
    experts = router.shape[2]
    n_tiles = n_expert // SPLIT
    bf16, f32 = jnp.bfloat16, jnp.float32
    tile_set = (STEPS, n_tiles, CAP, width)
    vmem = pltpu.VMEM
    return pl.pallas_call(
        functools.partial(kernel, n_section, n_expert),
        out_shape=jax.ShapeDtypeStruct(activations.shape, bf16),
        in_specs=[pl.BlockSpec(memory_space=pl.ANY)] * 7,
        out_specs=pl.BlockSpec(memory_space=pl.ANY),
        scratch_shapes=[
            vmem((STEPS + 1, TOK, width), bf16),
            vmem((1, width), f32),
            vmem((width, experts), bf16),
            vmem(expert_in.shape[2:], bf16),
            vmem(expert_down.shape[2:], bf16),
            vmem(expert_ids.shape, jnp.int32),
            vmem(slot_ids.shape, jnp.int32),
            vmem((TOK, width), bf16),
            vmem((STEPS, n_tiles, CAP, TOK), bf16),
            vmem((STEPS, TOK, TOK), f32),
            vmem((STEPS, n_tiles, CAP, TOK), bf16),
            vmem((STEPS, TOK, TOK), f32),
            vmem((STEPS, TOK, width), bf16),
            vmem(tile_set, bf16),
            vmem((STEPS, SPLIT, n_tiles, CAP, width), bf16),
            vmem((STEPS, SPLIT, n_tiles, CAP, width), bf16),
            vmem(tile_set, bf16),
            vmem(tile_set, bf16),
            vmem(tile_set, bf16),
            vmem(tile_set, bf16),
            vmem(tile_set, bf16),
            vmem(tile_set, bf16),
            vmem((TOK, width), f32),
            pltpu.SemaphoreType.DMA((7,)),
            pltpu.SemaphoreType.DMA((STEPS, 9, n_tiles)),
            pltpu.SemaphoreType.DMA((STEPS, 9, n_tiles)),
        ],
        compiler_params=pltpu.CompilerParams(
            collective_id=0, has_side_effects=True, vmem_limit_bytes=58 * 1024 * 1024
        ),
        cost_estimate=pl.CostEstimate(flops=5_000_000_000, bytes_accessed=5_000_000, transcendentals=800_000),
    )(activations, norm_gain, router, expert_in, expert_down, expert_ids, slot_ids)


def solution(mesh):
    in_specs = (
        P("section", "expert", None),
        P("section", None),
        P("section", None, None),
        P("section", "expert", None, None),
        P("section", "expert", None, None),
        P(None, "section", "expert"),
        P(None, "section", "expert"),
    )
    body = functools.partial(local, mesh.shape["section"], mesh.shape["expert"])
    return jax.shard_map(body, mesh=mesh, in_specs=in_specs, out_specs=P("section", "expert", None), check_vma=False)
```

```python
import functools

import jax
import jax.numpy as jnp
from jax import lax
from jax.experimental import pallas as pl
from jax.experimental.pallas import tpu as pltpu
from jax.sharding import PartitionSpec as P

STEPS = 2
PAIR = 2
OFFSET = 4
ORDER = "ABSCDEG"
CAP = 24
TOK = 128
SPLIT = 4
MESH = pl.DeviceIdType.MESH
LAND, TO_SIBLING, TO_PARTNER, TO_BOTH, PART_SIBLING, PART_FAR, PART_PARTNER, RESULT, META = range(9)


def kernel(
    n_section, n_expert,
    x_ref, gain_ref, router_ref, w_in_ref, w_down_ref, ids_ref, slots_ref,
    out_ref,
    x_buf, gain, router, w_in, w_down, ids, slots,
    normed, onehot, weight, onehot_in, weight_in, x_in,
    tiles, rows, part, far_in, sib_in, pair_in, pair_out, final, result,
    gathered, local_sem, send_sem, recv_sem,
):
    f32, bf16 = jnp.float32, jnp.bfloat16
    chips = n_expert // 2
    n_tiles = n_expert // SPLIT
    width = x_buf.shape[2]
    hidden_width = w_down.shape[0]
    s = lax.axis_index("section")
    e = lax.axis_index("expert")
    z, c = e // 2, e % 2
    side = z % 2
    s_next = (s + 1) % n_section
    s_prev = (s + n_section - 1) % n_section

    def source(k):
        return (z + (2 * side - 1) * k + chips) % chips

    def target(k):
        return (z + (1 - 2 * ((z + k) % 2)) * k + chips) % chips

    sibling = (s, e + 1 - 2 * c)
    partner = (s, (z + 1 - 2 * side) * 2 + c)

    loads = [
        pltpu.make_async_copy(x_ref.at[0], x_buf.at[0], local_sem.at[0]),
        pltpu.make_async_copy(gain_ref, gain, local_sem.at[1]),
        pltpu.make_async_copy(router_ref.at[0], router, local_sem.at[2]),
        pltpu.make_async_copy(ids_ref, ids, local_sem.at[3]),
        pltpu.make_async_copy(slots_ref, slots, local_sem.at[4]),
        pltpu.make_async_copy(w_in_ref.at[0, 0], w_in, local_sem.at[5]),
        pltpu.make_async_copy(w_down_ref.at[0, 0], w_down, local_sem.at[6]),
    ]
    for load in loads:
        load.start()

    barrier = pltpu.get_barrier_semaphore()

    def greet(device):
        pl.semaphore_signal(barrier, inc=1, device_id=device, device_id_type=MESH)

    greet(sibling)
    greet(partner)

    @pl.loop(0, n_tiles)
    def _(k):
        greet((s_next, source(k) * 2 + c))
        greet((s_prev, target(k) * 2 + c))

    @pl.loop(1, n_tiles)
    def _(k):
        greet((s, source(k) * 2 + c))
        greet((s, target(k) * 2 + c))

    for load in loads[:5]:
        load.wait()

    groups = n_tiles // PAIR
    period = groups + 6

    def some(q):
        return pl.ds(q * PAIR, PAIR)

    def remote(t, kind, k, src, dst, device):
        return pltpu.make_async_remote_copy(
            src_ref=src, dst_ref=dst, send_sem=send_sem.at[t, kind, k], recv_sem=recv_sem.at[t, kind, k],
            device_id=device, device_id_type=MESH,
        )

    def land(t, k):
        return remote(t, LAND, k, tiles.at[t, k], rows.at[t, 0, k], (s, target(k) * 2 + c))

    def to_sibling(t, q):
        return remote(t, TO_SIBLING, q, rows.at[t, 0, some(q)], rows.at[t, 1, some(q)], sibling)

    def to_partner(t, q):
        return remote(t, TO_PARTNER, q, rows.at[t, 0, some(q)], rows.at[t, 2, some(q)], partner)

    def to_both(t, q):
        return remote(t, TO_BOTH, q, rows.at[t, 2, some(q)], rows.at[t, 3, some(q)], sibling)

    def part_sibling(t, q):
        return remote(t, PART_SIBLING, q, part.at[t, 1, some(q)], sib_in.at[t, some(q)], sibling)

    def part_far(t, q):
        return remote(t, PART_FAR, q, part.at[t, 3, some(q)], far_in.at[t, some(q)], sibling)

    def part_partner(t, q):
        return remote(t, PART_PARTNER, q, pair_out.at[t, some(q)], pair_in.at[t, some(q)], partner)

    def to_home(t, k):
        return remote(t, RESULT, k, final.at[t, k], result.at[t, k], (s_next, source(k) * 2 + c))

    def meta(t, which):
        src, dst = ((x_buf, x_in), (weight, weight_in), (onehot, onehot_in))[which]
        return remote(t, META, which, src.at[t], dst.at[t], (s_next, e))

    def prepare(t):
        for i in range(TOK // 16):
            at = pl.ds(i * 16, 16)
            wide = x_buf[t, at, :].astype(f32)
            inverse = lax.rsqrt(jnp.mean(wide * wide, axis=-1, keepdims=True) + 1e-06)
            normed[at, :] = (wide * inverse * gain[...]).astype(bf16)

        row_of = ids[t] * CAP + slots[t]
        for k in range(n_tiles):
            place = lax.broadcasted_iota(jnp.int32, (CAP, TOK), 0) + (target(k) // 2) * CAP
            onehot[t, k] = jnp.where(place == row_of, 1.0, 0.0).astype(bf16)

    def dispatch(t):
        def scattered(k):
            return jnp.dot(onehot[t, k], normed[...], preferred_element_type=f32).astype(bf16)

        @pl.loop(1, n_tiles)
        def _(k):
            tiles[t, k] = scattered(k)
            land(t, k).start()

        rows[t, 0, 0] = scattered(0)

        logits = lax.dot_general(
            router[...], normed[...], (((1,), (1,)), ((), ())), preferred_element_type=f32
        )
        expert = lax.broadcasted_iota(jnp.int32, logits.shape, 0)
        picked = jnp.sum(jnp.where(expert == ids[t], logits, 0.0), axis=0, keepdims=True)
        weight[t] = jnp.transpose(jnp.broadcast_to(jax.nn.sigmoid(picked), (TOK, TOK)))
        for which in range(3):
            meta(t, which).start()

    def experts(t, members, q):
        held = jnp.concatenate(
            [rows[t, g, q * PAIR + a].astype(f32) for g in members for a in range(PAIR)], axis=0
        ).astype(bf16)
        projected = jnp.dot(held, w_in[...], preferred_element_type=f32)
        gate, up = projected[:, :hidden_width], projected[:, hidden_width:]
        hidden = (gate * jax.nn.sigmoid(gate) * up).astype(bf16)
        value = jnp.dot(hidden, w_down[...], preferred_element_type=f32)
        at = 0
        for g in members:
            for a in range(PAIR):
                part[t, g, q * PAIR + a] = value[at : at + CAP].astype(bf16)
                at += CAP

    def mix(t):
        for which in range(2):
            meta(t, which).wait_recv()
        for i in range(TOK // 16):
            at = pl.ds(i * 16, 16)
            mixed = x_in[t, at, :].astype(f32) + weight_in[t, at, 0:1] * gathered[at, :]
            x_buf[t + 1, at, :] = mixed.astype(bf16)

    def hand_on(t, q):
        for a in range(PAIR):
            k = q * PAIR + a

            @pl.when(k > 0)
            def _():
                land(t, k).wait_recv()

        to_partner(t, q).start()
        to_sibling(t, q).start()

    def hand_over(t, q):
        to_partner(t, q).wait_recv()
        to_both(t, q).start()

    def own_experts(t, q):
        experts(t, (0, 2), q)

    def sibling_experts(t, q):
        to_sibling(t, q).wait_recv()
        to_both(t, q).wait_recv()
        experts(t, (1, 3), q)
        part_far(t, q).start()
        part_sibling(t, q).start()

    def add_pair(t, q):
        part_far(t, q).wait_recv()
        for a in range(PAIR):
            k = q * PAIR + a
            pair_out[t, k] = (part[t, 2, k].astype(f32) + far_in[t, k].astype(f32)).astype(bf16)
        part_partner(t, q).start()

    def add_all(t, q):
        part_sibling(t, q).wait_recv()
        part_partner(t, q).wait_recv()
        for a in range(PAIR):
            k = q * PAIR + a
            total = part[t, 0, k].astype(f32) + sib_in[t, k].astype(f32) + pair_in[t, k].astype(f32)
            final[t, k] = total.astype(bf16)
            to_home(t, k).start()

    def gather(t, q):
        for a in range(PAIR):
            k = q * PAIR + a
            to_home(t, k).wait_recv()
            here = lax.dot_general(
                onehot_in[t, k], result[t, k], (((0,), (0,)), ((), ())), preferred_element_type=f32
            )
            if a == 0:
                @pl.when(k == 0)
                def _():
                    gathered[...] = here

                @pl.when(k > 0)
                def _():
                    gathered[...] += here
            else:
                gathered[...] += here

    own_turn = {
        "A": (hand_on, 0), "B": (hand_over, 1), "C": (own_experts, 2), "D": (add_pair, 3), "E": (add_all, 4),
        "G": (gather, 6),
    }

    prepare(0)
    for load in loads[5:]:
        load.wait()
    pl.semaphore_wait(barrier, 4 * n_tiles)

    @pl.loop(0, STEPS * period + OFFSET + 1)
    def _(turn):
        own = turn - 1 - c * OFFSET
        other = turn - 1 - (1 - c) * OFFSET

        def at_turn(action, index, delay):
            later = index + period
            t = later // period - 1
            q = later % period - delay

            @pl.when((index >= 0) & (t < STEPS) & (q >= 0) & (q < groups))
            def _():
                action(jnp.minimum(jnp.maximum(t, 0), STEPS - 1), jnp.minimum(jnp.maximum(q, 0), groups - 1))

        for name in ORDER:
            if name == "S":
                at_turn(sibling_experts, other, 2)
            else:
                action, delay = own_turn[name]
                if name == "G":
                    @pl.when((own >= 0) & (own < STEPS * period) & (own % period == 6))
                    def _():
                        meta(jnp.minimum(own // period, STEPS - 1), 2).wait_recv()

                at_turn(action, own, delay)

        upcoming = (own + 1 + period) // period - 1

        @pl.when((own >= 0) & (own % period == period - 1) & (upcoming <= STEPS))
        def _():
            mix(jnp.minimum(jnp.maximum(upcoming - 1, 0), STEPS - 1))

        @pl.when((own >= 0) & (own % period == period - 1) & (upcoming < STEPS))
        def _():
            prepare(jnp.minimum(jnp.maximum(upcoming, 0), STEPS - 1))

        @pl.when((own >= -1) & ((own + 1) % period == 0) & (upcoming < STEPS))
        def _():
            dispatch(jnp.minimum(jnp.maximum(upcoming, 0), STEPS - 1))

    store = pltpu.make_async_copy(x_buf.at[STEPS], out_ref.at[0], local_sem.at[0])
    store.start()

    @pl.loop(0, STEPS)
    def _(t):
        for which in range(3):
            meta(t, which).wait_send()

        @pl.loop(0, n_tiles)
        def _(k):
            @pl.when(k > 0)
            def _():
                land(t, k).wait_send()

            to_home(t, k).wait_send()

        @pl.loop(0, groups)
        def _(q):
            for copy in (to_sibling, to_partner, to_both, part_sibling, part_far, part_partner):
                copy(t, q).wait_send()

    store.wait()


def local(n_section, n_expert, activations, norm_gain, router, expert_in, expert_down, expert_ids, slot_ids):
    width = activations.shape[2]
    experts = router.shape[2]
    n_tiles = n_expert // SPLIT
    bf16, f32 = jnp.bfloat16, jnp.float32
    tile_set = (STEPS, n_tiles, CAP, width)
    vmem = pltpu.VMEM
    return pl.pallas_call(
        functools.partial(kernel, n_section, n_expert),
        out_shape=jax.ShapeDtypeStruct(activations.shape, bf16),
        in_specs=[pl.BlockSpec(memory_space=pl.ANY)] * 7,
        out_specs=pl.BlockSpec(memory_space=pl.ANY),
        scratch_shapes=[
            vmem((STEPS + 1, TOK, width), bf16),
            vmem((1, width), f32),
            vmem((experts, width), bf16),
            vmem(expert_in.shape[2:], bf16),
            vmem(expert_down.shape[2:], bf16),
            vmem(expert_ids.shape, jnp.int32),
            vmem(slot_ids.shape, jnp.int32),
            vmem((TOK, width), bf16),
            vmem((STEPS, n_tiles, CAP, TOK), bf16),
            vmem((STEPS, TOK, TOK), f32),
            vmem((STEPS, n_tiles, CAP, TOK), bf16),
            vmem((STEPS, TOK, TOK), f32),
            vmem((STEPS, TOK, width), bf16),
            vmem(tile_set, bf16),
            vmem((STEPS, SPLIT, n_tiles, CAP, width), bf16),
            vmem((STEPS, SPLIT, n_tiles, CAP, width), bf16),
            vmem(tile_set, bf16),
            vmem(tile_set, bf16),
            vmem(tile_set, bf16),
            vmem(tile_set, bf16),
            vmem(tile_set, bf16),
            vmem(tile_set, bf16),
            vmem((TOK, width), f32),
            pltpu.SemaphoreType.DMA((7,)),
            pltpu.SemaphoreType.DMA((STEPS, 9, n_tiles)),
            pltpu.SemaphoreType.DMA((STEPS, 9, n_tiles)),
        ],
        compiler_params=pltpu.CompilerParams(
            collective_id=0, has_side_effects=True, vmem_limit_bytes=58 * 1024 * 1024
        ),
        cost_estimate=pl.CostEstimate(flops=5_000_000_000, bytes_accessed=5_000_000, transcendentals=800_000),
    )(activations, norm_gain, jnp.swapaxes(router, 1, 2), expert_in, expert_down, expert_ids, slot_ids)


def solution(mesh):
    in_specs = (
        P("section", "expert", None),
        P("section", None),
        P("section", None, None),
        P("section", "expert", None, None),
        P("section", "expert", None, None),
        P(None, "section", "expert"),
        P(None, "section", "expert"),
    )
    body = functools.partial(local, mesh.shape["section"], mesh.shape["expert"])
    return jax.shard_map(body, mesh=mesh, in_specs=in_specs, out_specs=P("section", "expert", None), check_vma=False)
```

```python
import functools

import jax
import jax.numpy as jnp
from jax import lax
from jax.experimental import pallas as pl
from jax.experimental.pallas import tpu as pltpu
from jax.sharding import PartitionSpec as P

STEPS = 2
PAIR = 2
OFFSET = 5
TURN = {"A": 0, "B": 1, "S": 2, "C": 2, "D": 3, "E": 5, "G": 7}
ORDER = "ADBSCEG"
CAP = 24
TOK = 128
SPLIT = 4
MESH = pl.DeviceIdType.MESH
LAND, TO_SIBLING, TO_PARTNER, TO_BOTH, PART_SIBLING, PART_FAR, PART_PARTNER, RESULT, META = range(9)


def kernel(
    n_section, n_expert,
    x_ref, gain_ref, router_ref, w_in_ref, w_down_ref, ids_ref, slots_ref,
    out_ref,
    x_buf, gain, router, w_in, w_down, ids, slots,
    normed, onehot, weight, onehot_in, weight_in, x_in,
    tiles, rows, part, far_in, sib_in, pair_in, pair_out, final, result,
    gathered, local_sem, send_sem, recv_sem,
):
    f32, bf16 = jnp.float32, jnp.bfloat16
    chips = n_expert // 2
    n_tiles = n_expert // SPLIT
    width = x_buf.shape[2]
    hidden_width = w_down.shape[0]
    s = lax.axis_index("section")
    e = lax.axis_index("expert")
    z, c = e // 2, e % 2
    side = z % 2
    s_next = (s + 1) % n_section
    s_prev = (s + n_section - 1) % n_section

    def source(k):
        return (z + (2 * side - 1) * k + chips) % chips

    def target(k):
        return (z + (1 - 2 * ((z + k) % 2)) * k + chips) % chips

    sibling = (s, e + 1 - 2 * c)
    partner = (s, (z + 1 - 2 * side) * 2 + c)

    loads = [
        pltpu.make_async_copy(x_ref.at[0], x_buf.at[0], local_sem.at[0]),
        pltpu.make_async_copy(gain_ref, gain, local_sem.at[1]),
        pltpu.make_async_copy(router_ref.at[0], router, local_sem.at[2]),
        pltpu.make_async_copy(ids_ref, ids, local_sem.at[3]),
        pltpu.make_async_copy(slots_ref, slots, local_sem.at[4]),
        pltpu.make_async_copy(w_in_ref.at[0, 0], w_in, local_sem.at[5]),
        pltpu.make_async_copy(w_down_ref.at[0, 0], w_down, local_sem.at[6]),
    ]
    for load in loads[:5]:
        load.start()

    barrier = pltpu.get_barrier_semaphore()

    def greet(device):
        pl.semaphore_signal(barrier, inc=1, device_id=device, device_id_type=MESH)

    greet(sibling)
    greet(partner)

    @pl.loop(0, n_tiles)
    def _(k):
        greet((s_next, source(k) * 2 + c))
        greet((s_prev, target(k) * 2 + c))

    @pl.loop(1, n_tiles)
    def _(k):
        greet((s, source(k) * 2 + c))
        greet((s, target(k) * 2 + c))

    for load in loads[:5]:
        load.wait()
    for load in loads[5:]:
        load.start()

    groups = n_tiles // PAIR
    period = groups + TURN["G"]

    def remote(t, kind, k, src, dst, device):
        return pltpu.make_async_remote_copy(
            src_ref=src, dst_ref=dst, send_sem=send_sem.at[t, kind, k], recv_sem=recv_sem.at[t, kind, k],
            device_id=device, device_id_type=MESH,
        )

    def land(t, k):
        return remote(t, LAND, k, tiles.at[t, k], rows.at[t, 0, k], (s, target(k) * 2 + c))

    def to_sibling(t, k):
        return remote(t, TO_SIBLING, k, rows.at[t, 0, k], rows.at[t, 1, k], sibling)

    def to_partner(t, k):
        return remote(t, TO_PARTNER, k, rows.at[t, 0, k], rows.at[t, 2, k], partner)

    def to_both(t, k):
        return remote(t, TO_BOTH, k, rows.at[t, 2, k], rows.at[t, 3, k], sibling)

    def part_sibling(t, k):
        return remote(t, PART_SIBLING, k, part.at[t, 1, k], sib_in.at[t, k], sibling)

    def part_far(t, k):
        return remote(t, PART_FAR, k, part.at[t, 3, k], far_in.at[t, k], sibling)

    def part_partner(t, k):
        return remote(t, PART_PARTNER, k, pair_out.at[t, k], pair_in.at[t, k], partner)

    def to_home(t, k):
        return remote(t, RESULT, k, final.at[t, k], result.at[t, k], (s_next, source(k) * 2 + c))

    def meta(t, which):
        src, dst = ((x_buf, x_in), (weight, weight_in), (onehot, onehot_in))[which]
        return remote(t, META, which, src.at[t], dst.at[t], (s_next, e))

    def prepare(t):
        for i in range(TOK // 16):
            at = pl.ds(i * 16, 16)
            wide = x_buf[t, at, :].astype(f32)
            inverse = lax.rsqrt(jnp.mean(wide * wide, axis=-1, keepdims=True) + 1e-06)
            normed[at, :] = (wide * inverse * gain[...]).astype(bf16)

        row_of = ids[t] * CAP + slots[t]
        for k in range(n_tiles):
            place = lax.broadcasted_iota(jnp.int32, (CAP, TOK), 0) + (target(k) // 2) * CAP
            onehot[t, k] = jnp.where(place == row_of, 1.0, 0.0).astype(bf16)

    def dispatch(t):
        def scattered(k):
            return jnp.dot(onehot[t, k], normed[...], preferred_element_type=f32).astype(bf16)

        @pl.loop(1, n_tiles)
        def _(k):
            tiles[t, k] = scattered(k)
            land(t, k).start()

        rows[t, 0, 0] = scattered(0)

        logits = lax.dot_general(
            router[...], normed[...], (((1,), (1,)), ((), ())), preferred_element_type=f32
        )
        expert = lax.broadcasted_iota(jnp.int32, logits.shape, 0)
        picked = jnp.sum(jnp.where(expert == ids[t], logits, 0.0), axis=0, keepdims=True)
        weight[t] = jnp.transpose(jnp.broadcast_to(jax.nn.sigmoid(picked), (TOK, TOK)))
        for which in range(3):
            meta(t, which).start()

    def experts(t, members, q):
        held = jnp.concatenate(
            [rows[t, g, q * PAIR + a].astype(f32) for g in members for a in range(PAIR)], axis=0
        ).astype(bf16)
        projected = jnp.dot(held, w_in[...], preferred_element_type=f32)
        gate, up = projected[:, :hidden_width], projected[:, hidden_width:]
        hidden = (gate * jax.nn.sigmoid(gate) * up).astype(bf16)
        value = jnp.dot(hidden, w_down[...], preferred_element_type=f32)
        at = 0
        for g in members:
            for a in range(PAIR):
                part[t, g, q * PAIR + a] = value[at : at + CAP].astype(bf16)
                at += CAP

    def mix(t):
        for which in range(2):
            meta(t, which).wait_recv()
        for i in range(TOK // 16):
            at = pl.ds(i * 16, 16)
            mixed = x_in[t, at, :].astype(f32) + weight_in[t, at, 0:1] * gathered[at, :]
            x_buf[t + 1, at, :] = mixed.astype(bf16)

    def hand_on(t, q):
        for a in range(PAIR):
            k = q * PAIR + a

            @pl.when(k > 0)
            def _():
                land(t, k).wait_recv()

            to_partner(t, k).start()
            to_sibling(t, k).start()

    def hand_over(t, q):
        for a in range(PAIR):
            k = q * PAIR + a
            to_partner(t, k).wait_recv()
            to_both(t, k).start()

    def own_experts(t, q):
        experts(t, (0, 2), q)

    def sibling_experts(t, q):
        for a in range(PAIR):
            to_sibling(t, q * PAIR + a).wait_recv()
            to_both(t, q * PAIR + a).wait_recv()
        experts(t, (1, 3), q)
        for copy in (part_far, part_sibling):
            for a in range(PAIR):
                copy(t, q * PAIR + a).start()

    def add_pair(t, q):
        for a in range(PAIR):
            k = q * PAIR + a
            part_far(t, k).wait_recv()
            pair_out[t, k] = (part[t, 2, k].astype(f32) + far_in[t, k].astype(f32)).astype(bf16)
            part_partner(t, k).start()

    def add_all(t, q):
        for a in range(PAIR):
            k = q * PAIR + a
            part_sibling(t, k).wait_recv()
            part_partner(t, k).wait_recv()
            total = part[t, 0, k].astype(f32) + sib_in[t, k].astype(f32) + pair_in[t, k].astype(f32)
            final[t, k] = total.astype(bf16)
            to_home(t, k).start()

    def gather(t, q):
        for a in range(PAIR):
            k = q * PAIR + a
            to_home(t, k).wait_recv()
            here = lax.dot_general(
                onehot_in[t, k], result[t, k], (((0,), (0,)), ((), ())), preferred_element_type=f32
            )
            if a == 0:
                @pl.when(k == 0)
                def _():
                    gathered[...] = here

                @pl.when(k > 0)
                def _():
                    gathered[...] += here
            else:
                gathered[...] += here

    actions = {
        "A": hand_on, "B": hand_over, "C": own_experts, "S": sibling_experts, "D": add_pair, "E": add_all, "G": gather,
    }

    prepare(0)
    pl.semaphore_wait(barrier, 4 * n_tiles)

    @pl.loop(0, STEPS * period + OFFSET + 1)
    def _(turn):
        @pl.when(turn == 1)
        def _():
            for load in loads[5:]:
                load.wait()

        own = turn - 1 - c * OFFSET
        other = turn - 1 - (1 - c) * OFFSET

        def at_turn(action, index, delay):
            later = index + period
            t = later // period - 1
            q = later % period - delay

            @pl.when((index >= 0) & (t < STEPS) & (q >= 0) & (q < groups))
            def _():
                action(jnp.minimum(jnp.maximum(t, 0), STEPS - 1), jnp.minimum(jnp.maximum(q, 0), groups - 1))

        for name in ORDER:
            if name == "G":
                @pl.when((own >= 0) & (own < STEPS * period) & (own % period == TURN["G"]))
                def _():
                    meta(jnp.minimum(own // period, STEPS - 1), 2).wait_recv()

            at_turn(actions[name], other if name == "S" else own, TURN[name])

        upcoming = (own + 1 + period) // period - 1

        @pl.when((own >= 0) & (own % period == period - 1) & (upcoming <= STEPS))
        def _():
            mix(jnp.minimum(jnp.maximum(upcoming - 1, 0), STEPS - 1))

        @pl.when((own >= 0) & (own % period == period - 1) & (upcoming < STEPS))
        def _():
            prepare(jnp.minimum(jnp.maximum(upcoming, 0), STEPS - 1))

        @pl.when((own >= -1) & ((own + 1) % period == 0) & (upcoming < STEPS))
        def _():
            dispatch(jnp.minimum(jnp.maximum(upcoming, 0), STEPS - 1))

    store = pltpu.make_async_copy(x_buf.at[STEPS], out_ref.at[0], local_sem.at[0])
    store.start()

    @pl.loop(0, STEPS)
    def _(t):
        for which in range(3):
            meta(t, which).wait_send()

        @pl.loop(0, n_tiles)
        def _(k):
            @pl.when(k > 0)
            def _():
                land(t, k).wait_send()

            for copy in (to_sibling, to_partner, to_both, part_sibling, part_far, part_partner, to_home):
                copy(t, k).wait_send()

    store.wait()


def local(n_section, n_expert, activations, norm_gain, router, expert_in, expert_down, expert_ids, slot_ids):
    width = activations.shape[2]
    experts = router.shape[2]
    n_tiles = n_expert // SPLIT
    bf16, f32 = jnp.bfloat16, jnp.float32
    tile_set = (STEPS, n_tiles, CAP, width)
    vmem = pltpu.VMEM
    return pl.pallas_call(
        functools.partial(kernel, n_section, n_expert),
        out_shape=jax.ShapeDtypeStruct(activations.shape, bf16),
        in_specs=[pl.BlockSpec(memory_space=pl.ANY)] * 7,
        out_specs=pl.BlockSpec(memory_space=pl.ANY),
        scratch_shapes=[
            vmem((STEPS + 1, TOK, width), bf16),
            vmem((1, width), f32),
            vmem((experts, width), bf16),
            vmem(expert_in.shape[2:], bf16),
            vmem(expert_down.shape[2:], bf16),
            vmem(expert_ids.shape, jnp.int32),
            vmem(slot_ids.shape, jnp.int32),
            vmem((TOK, width), bf16),
            vmem((STEPS, n_tiles, CAP, TOK), bf16),
            vmem((STEPS, TOK, TOK), f32),
            vmem((STEPS, n_tiles, CAP, TOK), bf16),
            vmem((STEPS, TOK, TOK), f32),
            vmem((STEPS, TOK, width), bf16),
            vmem(tile_set, bf16),
            vmem((STEPS, SPLIT, n_tiles, CAP, width), bf16),
            vmem((STEPS, SPLIT, n_tiles, CAP, width), bf16),
            vmem(tile_set, bf16),
            vmem(tile_set, bf16),
            vmem(tile_set, bf16),
            vmem(tile_set, bf16),
            vmem(tile_set, bf16),
            vmem(tile_set, bf16),
            vmem((TOK, width), f32),
            pltpu.SemaphoreType.DMA((7,)),
            pltpu.SemaphoreType.DMA((STEPS, 9, n_tiles)),
            pltpu.SemaphoreType.DMA((STEPS, 9, n_tiles)),
        ],
        compiler_params=pltpu.CompilerParams(
            collective_id=0, has_side_effects=True, vmem_limit_bytes=58 * 1024 * 1024
        ),
        cost_estimate=pl.CostEstimate(flops=5_000_000_000, bytes_accessed=5_000_000, transcendentals=800_000),
    )(activations, norm_gain, jnp.swapaxes(router, 1, 2), expert_in, expert_down, expert_ids, slot_ids)


def solution(mesh):
    in_specs = (
        P("section", "expert", None),
        P("section", None),
        P("section", None, None),
        P("section", "expert", None, None),
        P("section", "expert", None, None),
        P(None, "section", "expert"),
        P(None, "section", "expert"),
    )
    body = functools.partial(local, mesh.shape["section"], mesh.shape["expert"])
    return jax.shard_map(body, mesh=mesh, in_specs=in_specs, out_specs=P("section", "expert", None), check_vma=False)
```

```python
import functools

import jax
import jax.numpy as jnp
from jax import lax
from jax.experimental import pallas as pl
from jax.experimental.pallas import tpu as pltpu
from jax.sharding import PartitionSpec as P

STEPS = 2
PAIR = 2
OFFSET = 6
TURN = {"A": 0, "B": 2, "S": 3, "C": 3, "D": 4, "E": 6, "G": 8}
ORDER = "ADBSCEG"
CAP = 24
TOK = 128
SPLIT = 4
MESH = pl.DeviceIdType.MESH
LAND, TO_SIBLING, TO_PARTNER, TO_BOTH, PART_SIBLING, PART_FAR, PART_PARTNER, RESULT, META = range(9)


def kernel(
    n_section, n_expert,
    x_ref, gain_ref, router_ref, w_in_ref, w_down_ref, ids_ref, slots_ref,
    out_ref,
    x_buf, gain, router, w_in, w_down, ids, slots,
    normed, onehot, weight, onehot_in, weight_in, x_in,
    tiles, rows, part, far_in, sib_in, pair_in, pair_out, final, result,
    gathered, local_sem, send_sem, recv_sem,
):
    f32, bf16 = jnp.float32, jnp.bfloat16
    chips = n_expert // 2
    n_tiles = n_expert // SPLIT
    width = x_buf.shape[2]
    hidden_width = w_down.shape[0]
    s = lax.axis_index("section")
    e = lax.axis_index("expert")
    z, c = e // 2, e % 2
    side = z % 2
    s_next = (s + 1) % n_section
    s_prev = (s + n_section - 1) % n_section

    def source(k):
        return (z + (2 * side - 1) * k + chips) % chips

    def target(k):
        return (z + (1 - 2 * ((z + k) % 2)) * k + chips) % chips

    sibling = (s, e + 1 - 2 * c)
    partner = (s, (z + 1 - 2 * side) * 2 + c)

    loads = [
        pltpu.make_async_copy(x_ref.at[0], x_buf.at[0], local_sem.at[0]),
        pltpu.make_async_copy(gain_ref, gain, local_sem.at[1]),
        pltpu.make_async_copy(router_ref.at[0], router, local_sem.at[2]),
        pltpu.make_async_copy(ids_ref, ids, local_sem.at[3]),
        pltpu.make_async_copy(slots_ref, slots, local_sem.at[4]),
        pltpu.make_async_copy(w_in_ref.at[0, 0], w_in, local_sem.at[5]),
        pltpu.make_async_copy(w_down_ref.at[0, 0], w_down, local_sem.at[6]),
    ]
    for load in loads[:5]:
        load.start()

    barrier = pltpu.get_barrier_semaphore()

    def greet(device):
        pl.semaphore_signal(barrier, inc=1, device_id=device, device_id_type=MESH)

    greet(sibling)
    greet(partner)

    @pl.loop(0, n_tiles)
    def _(k):
        greet((s_next, source(k) * 2 + c))
        greet((s_prev, target(k) * 2 + c))

    @pl.loop(1, n_tiles)
    def _(k):
        greet((s, source(k) * 2 + c))
        greet((s, target(k) * 2 + c))

    for load in loads[:5]:
        load.wait()
    for load in loads[5:]:
        load.start()

    groups = n_tiles // PAIR
    period = groups + TURN["G"]

    def remote(t, kind, k, src, dst, device):
        return pltpu.make_async_remote_copy(
            src_ref=src, dst_ref=dst, send_sem=send_sem.at[t, kind, k], recv_sem=recv_sem.at[t, kind, k],
            device_id=device, device_id_type=MESH,
        )

    def land(t, k):
        return remote(t, LAND, k, tiles.at[t, k], rows.at[t, 0, k], (s, target(k) * 2 + c))

    def to_sibling(t, k):
        return remote(t, TO_SIBLING, k, rows.at[t, 0, k], rows.at[t, 1, k], sibling)

    def to_partner(t, k):
        return remote(t, TO_PARTNER, k, rows.at[t, 0, k], rows.at[t, 2, k], partner)

    def to_both(t, k):
        return remote(t, TO_BOTH, k, rows.at[t, 2, k], rows.at[t, 3, k], sibling)

    def part_sibling(t, k):
        return remote(t, PART_SIBLING, k, part.at[t, 1, k], sib_in.at[t, k], sibling)

    def part_far(t, k):
        return remote(t, PART_FAR, k, part.at[t, 3, k], far_in.at[t, k], sibling)

    def part_partner(t, k):
        return remote(t, PART_PARTNER, k, pair_out.at[t, k], pair_in.at[t, k], partner)

    def to_home(t, k):
        return remote(t, RESULT, k, final.at[t, k], result.at[t, k], (s_next, source(k) * 2 + c))

    def meta(t, which):
        src, dst = ((x_buf, x_in), (weight, weight_in), (onehot, onehot_in))[which]
        return remote(t, META, which, src.at[t], dst.at[t], (s_next, e))

    def prepare(t):
        for i in range(TOK // 16):
            at = pl.ds(i * 16, 16)
            wide = x_buf[t, at, :].astype(f32)
            inverse = lax.rsqrt(jnp.mean(wide * wide, axis=-1, keepdims=True) + 1e-06)
            normed[at, :] = (wide * inverse * gain[...]).astype(bf16)

        row_of = ids[t] * CAP + slots[t]
        for k in range(n_tiles):
            place = lax.broadcasted_iota(jnp.int32, (CAP, TOK), 0) + (target(k) // 2) * CAP
            onehot[t, k] = jnp.where(place == row_of, 1.0, 0.0).astype(bf16)

    def dispatch(t):
        def scattered(k):
            return jnp.dot(onehot[t, k], normed[...], preferred_element_type=f32).astype(bf16)

        @pl.loop(1, n_tiles)
        def _(k):
            tiles[t, k] = scattered(k)
            land(t, k).start()

        rows[t, 0, 0] = scattered(0)

        logits = lax.dot_general(
            router[...], normed[...], (((1,), (1,)), ((), ())), preferred_element_type=f32
        )
        expert = lax.broadcasted_iota(jnp.int32, logits.shape, 0)
        picked = jnp.sum(jnp.where(expert == ids[t], logits, 0.0), axis=0, keepdims=True)
        weight[t] = jnp.transpose(jnp.broadcast_to(jax.nn.sigmoid(picked), (TOK, TOK)))
        for which in range(3):
            meta(t, which).start()

    def experts(t, members, q):
        held = jnp.concatenate(
            [rows[t, g, q * PAIR + a].astype(f32) for g in members for a in range(PAIR)], axis=0
        ).astype(bf16)
        projected = jnp.dot(held, w_in[...], preferred_element_type=f32)
        gate, up = projected[:, :hidden_width], projected[:, hidden_width:]
        hidden = (gate * jax.nn.sigmoid(gate) * up).astype(bf16)
        value = jnp.dot(hidden, w_down[...], preferred_element_type=f32)
        at = 0
        for g in members:
            for a in range(PAIR):
                part[t, g, q * PAIR + a] = value[at : at + CAP].astype(bf16)
                at += CAP

    def mix(t):
        for which in range(2):
            meta(t, which).wait_recv()
        for i in range(TOK // 16):
            at = pl.ds(i * 16, 16)
            mixed = x_in[t, at, :].astype(f32) + weight_in[t, at, 0:1] * gathered[at, :]
            x_buf[t + 1, at, :] = mixed.astype(bf16)

    def hand_on(t, q):
        for a in range(PAIR):
            k = q * PAIR + a

            @pl.when(k > 0)
            def _():
                land(t, k).wait_recv()

            to_partner(t, k).start()
            to_sibling(t, k).start()

    def hand_over(t, q):
        for a in range(PAIR):
            k = q * PAIR + a
            to_partner(t, k).wait_recv()
            to_both(t, k).start()

    def own_experts(t, q):
        experts(t, (0, 2), q)

    def sibling_experts(t, q):
        for a in range(PAIR):
            to_sibling(t, q * PAIR + a).wait_recv()
            to_both(t, q * PAIR + a).wait_recv()
        experts(t, (1, 3), q)
        for copy in (part_far, part_sibling):
            for a in range(PAIR):
                copy(t, q * PAIR + a).start()

    def add_pair(t, q):
        for a in range(PAIR):
            k = q * PAIR + a
            part_far(t, k).wait_recv()
            pair_out[t, k] = (part[t, 2, k].astype(f32) + far_in[t, k].astype(f32)).astype(bf16)
            part_partner(t, k).start()

    def add_all(t, q):
        for a in range(PAIR):
            k = q * PAIR + a
            part_sibling(t, k).wait_recv()
            part_partner(t, k).wait_recv()
            total = part[t, 0, k].astype(f32) + sib_in[t, k].astype(f32) + pair_in[t, k].astype(f32)
            final[t, k] = total.astype(bf16)
            to_home(t, k).start()

    def gather(t, q):
        for a in range(PAIR):
            k = q * PAIR + a
            to_home(t, k).wait_recv()
            here = lax.dot_general(
                onehot_in[t, k], result[t, k], (((0,), (0,)), ((), ())), preferred_element_type=f32
            )
            if a == 0:
                @pl.when(k == 0)
                def _():
                    gathered[...] = here

                @pl.when(k > 0)
                def _():
                    gathered[...] += here
            else:
                gathered[...] += here

    actions = {
        "A": hand_on, "B": hand_over, "C": own_experts, "S": sibling_experts, "D": add_pair, "E": add_all, "G": gather,
    }

    prepare(0)
    pl.semaphore_wait(barrier, 4 * n_tiles)

    @pl.loop(0, STEPS * period + OFFSET + 1)
    def _(turn):
        @pl.when(turn == 1)
        def _():
            for load in loads[5:]:
                load.wait()

        own = turn - 1 - c * OFFSET
        other = turn - 1 - (1 - c) * OFFSET

        def at_turn(action, index, delay):
            later = index + period
            t = later // period - 1
            q = later % period - delay

            @pl.when((index >= 0) & (t < STEPS) & (q >= 0) & (q < groups))
            def _():
                action(jnp.minimum(jnp.maximum(t, 0), STEPS - 1), jnp.minimum(jnp.maximum(q, 0), groups - 1))

        for name in ORDER:
            if name == "G":
                @pl.when((own >= 0) & (own < STEPS * period) & (own % period == TURN["G"]))
                def _():
                    meta(jnp.minimum(own // period, STEPS - 1), 2).wait_recv()

            at_turn(actions[name], other if name == "S" else own, TURN[name])

        upcoming = (own + 1 + period) // period - 1

        @pl.when((own >= 0) & (own % period == period - 1) & (upcoming <= STEPS))
        def _():
            mix(jnp.minimum(jnp.maximum(upcoming - 1, 0), STEPS - 1))

        @pl.when((own >= 0) & (own % period == period - 1) & (upcoming < STEPS))
        def _():
            prepare(jnp.minimum(jnp.maximum(upcoming, 0), STEPS - 1))

        @pl.when((own >= -1) & ((own + 1) % period == 0) & (upcoming < STEPS))
        def _():
            dispatch(jnp.minimum(jnp.maximum(upcoming, 0), STEPS - 1))

    store = pltpu.make_async_copy(x_buf.at[STEPS], out_ref.at[0], local_sem.at[0])
    store.start()

    @pl.loop(0, STEPS)
    def _(t):
        for which in range(3):
            meta(t, which).wait_send()

        @pl.loop(0, n_tiles)
        def _(k):
            @pl.when(k > 0)
            def _():
                land(t, k).wait_send()

            for copy in (to_sibling, to_partner, to_both, part_sibling, part_far, part_partner, to_home):
                copy(t, k).wait_send()

    store.wait()


def local(n_section, n_expert, activations, norm_gain, router, expert_in, expert_down, expert_ids, slot_ids):
    width = activations.shape[2]
    experts = router.shape[2]
    n_tiles = n_expert // SPLIT
    bf16, f32 = jnp.bfloat16, jnp.float32
    tile_set = (STEPS, n_tiles, CAP, width)
    vmem = pltpu.VMEM
    return pl.pallas_call(
        functools.partial(kernel, n_section, n_expert),
        out_shape=jax.ShapeDtypeStruct(activations.shape, bf16),
        in_specs=[pl.BlockSpec(memory_space=pl.ANY)] * 7,
        out_specs=pl.BlockSpec(memory_space=pl.ANY),
        scratch_shapes=[
            vmem((STEPS + 1, TOK, width), bf16),
            vmem((1, width), f32),
            vmem((experts, width), bf16),
            vmem(expert_in.shape[2:], bf16),
            vmem(expert_down.shape[2:], bf16),
            vmem(expert_ids.shape, jnp.int32),
            vmem(slot_ids.shape, jnp.int32),
            vmem((TOK, width), bf16),
            vmem((STEPS, n_tiles, CAP, TOK), bf16),
            vmem((STEPS, TOK, TOK), f32),
            vmem((STEPS, n_tiles, CAP, TOK), bf16),
            vmem((STEPS, TOK, TOK), f32),
            vmem((STEPS, TOK, width), bf16),
            vmem(tile_set, bf16),
            vmem((STEPS, SPLIT, n_tiles, CAP, width), bf16),
            vmem((STEPS, SPLIT, n_tiles, CAP, width), bf16),
            vmem(tile_set, bf16),
            vmem(tile_set, bf16),
            vmem(tile_set, bf16),
            vmem(tile_set, bf16),
            vmem(tile_set, bf16),
            vmem(tile_set, bf16),
            vmem((TOK, width), f32),
            pltpu.SemaphoreType.DMA((7,)),
            pltpu.SemaphoreType.DMA((STEPS, 9, n_tiles)),
            pltpu.SemaphoreType.DMA((STEPS, 9, n_tiles)),
        ],
        compiler_params=pltpu.CompilerParams(
            collective_id=0, has_side_effects=True, vmem_limit_bytes=58 * 1024 * 1024
        ),
        cost_estimate=pl.CostEstimate(flops=5_000_000_000, bytes_accessed=5_000_000, transcendentals=800_000),
    )(activations, norm_gain, jnp.swapaxes(router, 1, 2), expert_in, expert_down, expert_ids, slot_ids)


def solution(mesh):
    in_specs = (
        P("section", "expert", None),
        P("section", None),
        P("section", None, None),
        P("section", "expert", None, None),
        P("section", "expert", None, None),
        P(None, "section", "expert"),
        P(None, "section", "expert"),
    )
    body = functools.partial(local, mesh.shape["section"], mesh.shape["expert"])
    return jax.shard_map(body, mesh=mesh, in_specs=in_specs, out_specs=P("section", "expert", None), check_vma=False)
```

```python
import functools

import jax
import jax.numpy as jnp
from jax import lax
from jax.experimental import pallas as pl
from jax.experimental.pallas import tpu as pltpu
from jax.sharding import PartitionSpec as P

STEPS = 2
PAIR = 2
OFFSET = 7
TURN = {"A": 0, "B": 2, "S": 3, "C": 3, "D": 4, "E": 6, "G": 8}
ORDER = "ADBSCEG"
CAP = 24
TOK = 128
SPLIT = 4
MESH = pl.DeviceIdType.MESH
LAND, TO_SIBLING, TO_PARTNER, TO_BOTH, PART_SIBLING, PART_FAR, PART_PARTNER, RESULT, META = range(9)


def kernel(
    n_section, n_expert,
    x_ref, gain_ref, router_ref, w_in_ref, w_down_ref, ids_ref, slots_ref,
    out_ref,
    x_buf, gain, router, w_in, w_down, ids, slots,
    normed, onehot, weight, onehot_in, weight_in, x_in,
    tiles, rows, part, far_in, sib_in, pair_in, pair_out, final, result,
    gathered, local_sem, send_sem, recv_sem,
):
    f32, bf16 = jnp.float32, jnp.bfloat16
    chips = n_expert // 2
    n_tiles = n_expert // SPLIT
    width = x_buf.shape[2]
    hidden_width = w_down.shape[0]
    s = lax.axis_index("section")
    e = lax.axis_index("expert")
    z, c = e // 2, e % 2
    side = z % 2
    s_next = (s + 1) % n_section
    s_prev = (s + n_section - 1) % n_section

    def source(k):
        return (z + (2 * side - 1) * k + chips) % chips

    def target(k):
        return (z + (1 - 2 * ((z + k) % 2)) * k + chips) % chips

    sibling = (s, e + 1 - 2 * c)
    partner = (s, (z + 1 - 2 * side) * 2 + c)

    loads = [
        pltpu.make_async_copy(x_ref.at[0], x_buf.at[0], local_sem.at[0]),
        pltpu.make_async_copy(gain_ref, gain, local_sem.at[1]),
        pltpu.make_async_copy(router_ref.at[0], router, local_sem.at[2]),
        pltpu.make_async_copy(ids_ref, ids, local_sem.at[3]),
        pltpu.make_async_copy(slots_ref, slots, local_sem.at[4]),
        pltpu.make_async_copy(w_in_ref.at[0, 0], w_in, local_sem.at[5]),
        pltpu.make_async_copy(w_down_ref.at[0, 0], w_down, local_sem.at[6]),
    ]
    for load in loads[:5]:
        load.start()

    barrier = pltpu.get_barrier_semaphore()

    def greet(device):
        pl.semaphore_signal(barrier, inc=1, device_id=device, device_id_type=MESH)

    greet(sibling)
    greet(partner)

    @pl.loop(0, n_tiles)
    def _(k):
        greet((s_next, source(k) * 2 + c))
        greet((s_prev, target(k) * 2 + c))

    @pl.loop(1, n_tiles)
    def _(k):
        greet((s, source(k) * 2 + c))
        greet((s, target(k) * 2 + c))

    for load in loads[:5]:
        load.wait()
    for load in loads[5:]:
        load.start()

    groups = n_tiles // PAIR
    period = groups + TURN["G"]

    def remote(t, kind, k, src, dst, device):
        return pltpu.make_async_remote_copy(
            src_ref=src, dst_ref=dst, send_sem=send_sem.at[t, kind, k], recv_sem=recv_sem.at[t, kind, k],
            device_id=device, device_id_type=MESH,
        )

    def land(t, k):
        return remote(t, LAND, k, tiles.at[t, k], rows.at[t, 0, k], (s, target(k) * 2 + c))

    def to_sibling(t, k):
        return remote(t, TO_SIBLING, k, rows.at[t, 0, k], rows.at[t, 1, k], sibling)

    def to_partner(t, k):
        return remote(t, TO_PARTNER, k, rows.at[t, 0, k], rows.at[t, 2, k], partner)

    def to_both(t, k):
        return remote(t, TO_BOTH, k, rows.at[t, 2, k], rows.at[t, 3, k], sibling)

    def part_sibling(t, k):
        return remote(t, PART_SIBLING, k, part.at[t, 1, k], sib_in.at[t, k], sibling)

    def part_far(t, k):
        return remote(t, PART_FAR, k, part.at[t, 3, k], far_in.at[t, k], sibling)

    def part_partner(t, k):
        return remote(t, PART_PARTNER, k, pair_out.at[t, k], pair_in.at[t, k], partner)

    def to_home(t, k):
        return remote(t, RESULT, k, final.at[t, k], result.at[t, k], (s_next, source(k) * 2 + c))

    def meta(t, which):
        src, dst = ((x_buf, x_in), (weight, weight_in), (onehot, onehot_in))[which]
        return remote(t, META, which, src.at[t], dst.at[t], (s_next, e))

    def prepare(t):
        for i in range(TOK // 16):
            at = pl.ds(i * 16, 16)
            wide = x_buf[t, at, :].astype(f32)
            inverse = lax.rsqrt(jnp.mean(wide * wide, axis=-1, keepdims=True) + 1e-06)
            normed[at, :] = (wide * inverse * gain[...]).astype(bf16)

        row_of = ids[t] * CAP + slots[t]
        for k in range(n_tiles):
            place = lax.broadcasted_iota(jnp.int32, (CAP, TOK), 0) + (target(k) // 2) * CAP
            onehot[t, k] = jnp.where(place == row_of, 1.0, 0.0).astype(bf16)

    def dispatch(t):
        def scattered(k):
            return jnp.dot(onehot[t, k], normed[...], preferred_element_type=f32).astype(bf16)

        @pl.loop(1, n_tiles)
        def _(k):
            tiles[t, k] = scattered(k)
            land(t, k).start()

        rows[t, 0, 0] = scattered(0)

        logits = lax.dot_general(
            router[...], normed[...], (((1,), (1,)), ((), ())), preferred_element_type=f32
        )
        expert = lax.broadcasted_iota(jnp.int32, logits.shape, 0)
        picked = jnp.sum(jnp.where(expert == ids[t], logits, 0.0), axis=0, keepdims=True)
        weight[t] = jnp.transpose(jnp.broadcast_to(jax.nn.sigmoid(picked), (TOK, TOK)))
        for which in range(3):
            meta(t, which).start()

    def experts(t, members, q):
        held = jnp.concatenate(
            [rows[t, g, q * PAIR + a].astype(f32) for g in members for a in range(PAIR)], axis=0
        ).astype(bf16)
        projected = jnp.dot(held, w_in[...], preferred_element_type=f32)
        gate, up = projected[:, :hidden_width], projected[:, hidden_width:]
        hidden = (gate * jax.nn.sigmoid(gate) * up).astype(bf16)
        value = jnp.dot(hidden, w_down[...], preferred_element_type=f32)
        at = 0
        for g in members:
            for a in range(PAIR):
                part[t, g, q * PAIR + a] = value[at : at + CAP].astype(bf16)
                at += CAP

    def mix(t):
        for which in range(2):
            meta(t, which).wait_recv()
        for i in range(TOK // 16):
            at = pl.ds(i * 16, 16)
            mixed = x_in[t, at, :].astype(f32) + weight_in[t, at, 0:1] * gathered[at, :]
            x_buf[t + 1, at, :] = mixed.astype(bf16)

    def hand_on(t, q):
        for a in range(PAIR):
            k = q * PAIR + a

            @pl.when(k > 0)
            def _():
                land(t, k).wait_recv()

            to_partner(t, k).start()
            to_sibling(t, k).start()

    def hand_over(t, q):
        for a in range(PAIR):
            k = q * PAIR + a
            to_partner(t, k).wait_recv()
            to_both(t, k).start()

    def own_experts(t, q):
        experts(t, (0, 2), q)

    def sibling_experts(t, q):
        for a in range(PAIR):
            to_sibling(t, q * PAIR + a).wait_recv()
            to_both(t, q * PAIR + a).wait_recv()
        experts(t, (1, 3), q)
        for copy in (part_far, part_sibling):
            for a in range(PAIR):
                copy(t, q * PAIR + a).start()

    def add_pair(t, q):
        for a in range(PAIR):
            k = q * PAIR + a
            part_far(t, k).wait_recv()
            pair_out[t, k] = (part[t, 2, k].astype(f32) + far_in[t, k].astype(f32)).astype(bf16)
            part_partner(t, k).start()

    def add_all(t, q):
        for a in range(PAIR):
            k = q * PAIR + a
            part_sibling(t, k).wait_recv()
            part_partner(t, k).wait_recv()
            total = part[t, 0, k].astype(f32) + sib_in[t, k].astype(f32) + pair_in[t, k].astype(f32)
            final[t, k] = total.astype(bf16)
            to_home(t, k).start()

    def gather(t, q):
        for a in range(PAIR):
            k = q * PAIR + a
            to_home(t, k).wait_recv()
            here = lax.dot_general(
                onehot_in[t, k], result[t, k], (((0,), (0,)), ((), ())), preferred_element_type=f32
            )
            if a == 0:
                @pl.when(k == 0)
                def _():
                    gathered[...] = here

                @pl.when(k > 0)
                def _():
                    gathered[...] += here
            else:
                gathered[...] += here

    actions = {
        "A": hand_on, "B": hand_over, "C": own_experts, "S": sibling_experts, "D": add_pair, "E": add_all, "G": gather,
    }

    prepare(0)
    pl.semaphore_wait(barrier, 4 * n_tiles)

    @pl.loop(0, STEPS * period + OFFSET + 1)
    def _(turn):
        @pl.when(turn == 1)
        def _():
            for load in loads[5:]:
                load.wait()

        own = turn - 1 - c * OFFSET
        other = turn - 1 - (1 - c) * OFFSET

        def at_turn(action, index, delay):
            later = index + period
            t = later // period - 1
            q = later % period - delay

            @pl.when((index >= 0) & (t < STEPS) & (q >= 0) & (q < groups))
            def _():
                action(jnp.minimum(jnp.maximum(t, 0), STEPS - 1), jnp.minimum(jnp.maximum(q, 0), groups - 1))

        for name in ORDER:
            if name == "G":
                @pl.when((own >= 0) & (own < STEPS * period) & (own % period == TURN["G"]))
                def _():
                    meta(jnp.minimum(own // period, STEPS - 1), 2).wait_recv()

            at_turn(actions[name], other if name == "S" else own, TURN[name])

        upcoming = (own + 1 + period) // period - 1

        @pl.when((own >= 0) & (own % period == period - 1) & (upcoming <= STEPS))
        def _():
            mix(jnp.minimum(jnp.maximum(upcoming - 1, 0), STEPS - 1))

        @pl.when((own >= 0) & (own % period == period - 1) & (upcoming < STEPS))
        def _():
            prepare(jnp.minimum(jnp.maximum(upcoming, 0), STEPS - 1))

        @pl.when((own >= -1) & ((own + 1) % period == 0) & (upcoming < STEPS))
        def _():
            dispatch(jnp.minimum(jnp.maximum(upcoming, 0), STEPS - 1))

    store = pltpu.make_async_copy(x_buf.at[STEPS], out_ref.at[0], local_sem.at[0])
    store.start()

    @pl.loop(0, STEPS)
    def _(t):
        for which in range(3):
            meta(t, which).wait_send()

        @pl.loop(0, n_tiles)
        def _(k):
            @pl.when(k > 0)
            def _():
                land(t, k).wait_send()

            for copy in (to_sibling, to_partner, to_both, part_sibling, part_far, part_partner, to_home):
                copy(t, k).wait_send()

    store.wait()


def local(n_section, n_expert, activations, norm_gain, router, expert_in, expert_down, expert_ids, slot_ids):
    width = activations.shape[2]
    experts = router.shape[2]
    n_tiles = n_expert // SPLIT
    bf16, f32 = jnp.bfloat16, jnp.float32
    tile_set = (STEPS, n_tiles, CAP, width)
    vmem = pltpu.VMEM
    return pl.pallas_call(
        functools.partial(kernel, n_section, n_expert),
        out_shape=jax.ShapeDtypeStruct(activations.shape, bf16),
        in_specs=[pl.BlockSpec(memory_space=pl.ANY)] * 7,
        out_specs=pl.BlockSpec(memory_space=pl.ANY),
        scratch_shapes=[
            vmem((STEPS + 1, TOK, width), bf16),
            vmem((1, width), f32),
            vmem((experts, width), bf16),
            vmem(expert_in.shape[2:], bf16),
            vmem(expert_down.shape[2:], bf16),
            vmem(expert_ids.shape, jnp.int32),
            vmem(slot_ids.shape, jnp.int32),
            vmem((TOK, width), bf16),
            vmem((STEPS, n_tiles, CAP, TOK), bf16),
            vmem((STEPS, TOK, TOK), f32),
            vmem((STEPS, n_tiles, CAP, TOK), bf16),
            vmem((STEPS, TOK, TOK), f32),
            vmem((STEPS, TOK, width), bf16),
            vmem(tile_set, bf16),
            vmem((STEPS, SPLIT, n_tiles, CAP, width), bf16),
            vmem((STEPS, SPLIT, n_tiles, CAP, width), bf16),
            vmem(tile_set, bf16),
            vmem(tile_set, bf16),
            vmem(tile_set, bf16),
            vmem(tile_set, bf16),
            vmem(tile_set, bf16),
            vmem(tile_set, bf16),
            vmem((TOK, width), f32),
            pltpu.SemaphoreType.DMA((7,)),
            pltpu.SemaphoreType.DMA((STEPS, 9, n_tiles)),
            pltpu.SemaphoreType.DMA((STEPS, 9, n_tiles)),
        ],
        compiler_params=pltpu.CompilerParams(
            collective_id=0, has_side_effects=True, vmem_limit_bytes=58 * 1024 * 1024
        ),
        cost_estimate=pl.CostEstimate(flops=5_000_000_000, bytes_accessed=5_000_000, transcendentals=800_000),
    )(activations, norm_gain, jnp.swapaxes(router, 1, 2), expert_in, expert_down, expert_ids, slot_ids)


def solution(mesh):
    in_specs = (
        P("section", "expert", None),
        P("section", None),
        P("section", None, None),
        P("section", "expert", None, None),
        P("section", "expert", None, None),
        P(None, "section", "expert"),
        P(None, "section", "expert"),
    )
    body = functools.partial(local, mesh.shape["section"], mesh.shape["expert"])
    return jax.shard_map(body, mesh=mesh, in_specs=in_specs, out_specs=P("section", "expert", None), check_vma=False)
```
